32 devices in a mesh: treated: 4 (over y, x), control: 8 (over z, core).
Axes of the slice: x: 2, y: 2, z: 4, core: 2. Of those that a mesh axis runs over, the one named last changes fastest.
Arguments:
- treated_emb: bfloat16 [4096, 1024], P(('treated', 'control')), may hold values from -20 to 20
- control_emb: bfloat16 [16384, 1024], P('control'), may hold values from -20 to 20
- control_pot: float32 [16384], P('control'), may hold values from -6 to 6
- control_logw: float32 [16384], P('control'), may hold values from -1.5 to 1.5
- treated_logw: float32 [4096], P('treated'), may hold values from -1.5 to 1.5
Outputs:
- treated_pot: float32 [4096], P('treated')
- column_lse: float32 [16384], P('control')
The draws below stay inside these ranges and needn't reach their ends.
All inputs are finite; a program needn't handle non-finite values.
Results may differ from the reference program's by a relative error of at most 0.0003.
Values may be sent and summed in bfloat16 or wider, within the bound.
No kernel may reach another device: no remote copies, remote signals or barrier semaphores. Data moves between devices by JAX's collectives and lax.ppermute only.
A program may use at most 64 MiB of HBM per device.

```python
import jax
import jax.numpy as jnp
from jax import lax

D = 1024
CC_DEV = 2048
NT = 4096
NC = 16384


def shared_embeddings(key):
    key_treated, key_control = jax.random.split(key)
    treated = jnp.clip(jax.random.normal(key_treated, (NT, D), jnp.float32), -5.0, 5.0)
    control = jnp.clip(jax.random.normal(key_control, (NC, D), jnp.float32), -5.0, 5.0)
    return (treated, control)


def draw_treated_emb(key, part):
    treated, control = shared_embeddings(key)
    return treated.astype(jnp.bfloat16)


def draw_control_emb(key, part):
    treated, control = shared_embeddings(key)
    return control.astype(jnp.bfloat16)


def block_scale(stream_key, dims, cuts, least, high):
    gain, own = 1.0, jax.random.fold_in(stream_key, 6)
    for position, parts in cuts:
        steps = jnp.exp(jax.random.uniform(jax.random.fold_in(own, position), (parts,), jnp.float32, least / len(cuts), high / len(cuts)))
        gain = gain * jnp.repeat(steps, dims[position] // parts).reshape([-1 if axis == position else 1 for axis in range(len(dims))])
    return gain


def bell_draw(stream_key, extent, width, reach, cuts=(), kind=jnp.bfloat16):
    array = jax.random.normal(stream_key, extent, jnp.float32) * width
    if len(cuts) > 0:
        array = block_scale(stream_key, extent, cuts, -0.22, 0.18) * array
    return jnp.clip(array, min=-reach, max=reach).astype(kind)


def setup_inputs(seed: int = 0) -> dict:
    seeds = jax.random.split(jax.random.key(seed), 6)
    return {
        "treated_emb": draw_treated_emb(jax.random.fold_in(seeds[5], 71), 0),
        "control_emb": draw_control_emb(jax.random.fold_in(seeds[5], 71), 0),
        "control_pot": bell_draw(seeds[2], (NC,), 1.0, 6.0, ((0, 8),), jnp.float32),
        "control_logw": jnp.clip(jax.random.uniform(seeds[3], (NC,), jnp.float32, -1.5, 1.5) * block_scale(seeds[3], (NC,), ((0, 8),), -0.4, 0.0), -1.5, 1.5),
        "treated_logw": jnp.clip(jax.random.uniform(seeds[4], (NT,), jnp.float32, -1.5, 1.5) * block_scale(seeds[4], (NT,), ((0, 4),), -0.4, 0.0), -1.5, 1.5),
    }


smoothing = 0.1


def scaled_cost(slab, slab_sq, block):
    cross = jnp.dot(slab, block.T, precision=lax.Precision.HIGHEST, preferred_element_type=jnp.float32)
    block_sq = jnp.sum(block * block, axis=1)
    return (slab_sq[:, None] + block_sq[None, :] - 2.0 * cross) / (D * smoothing)


def reference(treated_emb, control_emb, control_pot, control_logw, treated_logw):
    slab = treated_emb.astype(jnp.float32)
    slab_sq = jnp.sum(slab * slab, axis=1)
    blocks = control_emb.reshape(NC // CC_DEV, CC_DEV, D)
    biases = (control_pot + control_logw).reshape(NC // CC_DEV, CC_DEV)

    def row_step(carry, inputs):
        block, bias = inputs
        scores = bias[None, :] - scaled_cost(slab, slab_sq, block.astype(jnp.float32))
        highest = jnp.maximum(carry[0], jnp.max(scores, axis=1))
        total = carry[1] * jnp.exp(carry[0] - highest) + jnp.sum(jnp.exp(scores - highest[:, None]), axis=1)
        return (highest, total), None

    start = (jnp.full((NT,), -jnp.inf, jnp.float32), jnp.zeros((NT,), jnp.float32))
    (highest, total), unused = lax.scan(row_step, start, (blocks, biases))
    treated_pot = -(highest + jnp.log(total))
    row_bias = treated_pot + treated_logw

    def column_block(block):
        scores = row_bias[:, None] - scaled_cost(slab, slab_sq, block.astype(jnp.float32))
        summit = jnp.max(scores, axis=0)
        return summit + jnp.log(jnp.sum(jnp.exp(scores - summit[None, :]), axis=0))

    column_lse = lax.map(column_block, blocks).reshape(NC)
    return treated_pot, column_lse
```

```python
import functools

import jax
import jax.numpy as jnp
from jax import lax
from jax.experimental import pallas as pl
from jax.experimental.pallas import tpu as pltpu
from jax.sharding import PartitionSpec as P

smoothing = 0.1
LOG2E = 1.4426950408889634
LN2 = 0.6931471805599453
LARGE = 2.0**30
SMALL = 2.0**-50
MIB = 1024 * 1024
NT_DIMS = (((1,), (1,)), ((), ()))
WHOLE = pl.BlockSpec(memory_space=pltpu.VMEM)


def params(limit):
    return pltpu.CompilerParams(vmem_limit_bytes=limit * MIB)


def canonical(held, piece):
    if held is None:
        return piece
    chips, places = held
    me = lax.axis_index("control")
    shift, flip = places[piece]
    return (me // 2 + chips - shift) % chips * 2 + (me % 2 + flip) % 2


def log2_sum(parts):
    top = functools.reduce(jnp.maximum, parts)
    return top + jnp.log2(functools.reduce(jnp.add, [jnp.exp2(p - top) for p in parts]))


def turned(column):
    return jnp.transpose(jnp.broadcast_to(column, (128, 128)))[0:1, :]


def tree_sum(parts):
    while len(parts) > 1:
        parts = [functools.reduce(jnp.add, parts[i:i + 2]) for i in range(0, len(parts), 2)]
    return parts[0]


def folded(wide):
    return functools.reduce(jnp.add, [wide[:, j:j + 128] for j in range(0, wide.shape[1], 128)])


def scaled_product(x, y, scale):
    return lax.dot_general(x, y, NT_DIMS, preferred_element_type=jnp.float32) * scale


def chunk_kernel(scale, parts, earlier, held, *refs):
    x_refs, refs = refs[:parts], refs[parts:]
    y_ref, u_ref, refs = refs[0], refs[1], refs[2:]
    lse_refs, (e_ref, top_ref, lse_ref, wide_ref) = refs[:earlier], refs[earlier:]
    columns = y_ref.shape[0]
    x = jnp.concatenate([r[...] for r in x_refs], axis=0)
    rows = x.shape[0]
    tile = 256
    before = [r[h:h + 1, :] for r in lse_refs for h in range(r.shape[0])]

    def emit(top, total):
        own, sums = [], []
        for h in range(0, rows, 128):
            shift = turned(top[h:h + 128])
            row = jnp.sum(jnp.transpose(total[h:h + 128]), axis=0, keepdims=True)
            top_ref[h // 128:h // 128 + 1, :] = shift
            own.append(shift + jnp.log2(row))
            sums.append(row)
        for h, row in enumerate(before + own):
            if earlier:
                lse_ref[pl.ds(canonical(held, h), 1), :] = row
            else:
                lse_ref[h:h + 1, :] = row
        return functools.reduce(jnp.maximum, sums)

    top, total = None, None
    for j in range(0, columns, tile):
        t = scaled_product(x, y_ref[j:j + tile, :], scale) + u_ref[:, j:j + tile]
        if top is None:
            top = jnp.max(t, axis=1, keepdims=True)
        e = jnp.exp2(t - top)
        e_ref[:, j:j + tile] = e
        total = folded(e) if total is None else total + folded(e)
    largest = emit(top, total)

    @pl.when(jnp.logical_not(jnp.max(largest) < LARGE))
    def _():
        def scores(j):
            place = pl.ds(pl.multiple_of(j * tile, tile), tile)
            return place, scaled_product(x, y_ref[place, :], scale) + u_ref[:, place]

        wide_ref[...] = jnp.full_like(wide_ref, -jnp.inf)

        @pl.loop(0, columns // tile)
        def _(j):
            wide_ref[...] = jnp.maximum(wide_ref[...], jnp.max(scores(j)[1], axis=1, keepdims=True))

        top = wide_ref[:, 0:1]
        wide_ref[...] = jnp.zeros_like(wide_ref)

        @pl.loop(0, columns // tile)
        def _(j):
            place, t = scores(j)
            e = jnp.exp2(t - top)
            e_ref[:, place] = e
            wide_ref[...] += folded(e)

        emit(top, wide_ref[...])


def chunk_call(xs, y, u, held=None, lses=()):
    parts = len(xs)
    width = xs[0].shape[1]
    columns = y.shape[0]
    rows = sum(x.shape[0] for x in xs)
    scale = 2.0 * LOG2E / (width * smoothing)
    listed = rows // 128 + sum(a.shape[0] for a in lses)
    return pl.pallas_call(
        functools.partial(chunk_kernel, scale, parts, len(lses), held),
        in_specs=[WHOLE] * (parts + 2 + len(lses)),
        out_specs=[WHOLE, WHOLE, WHOLE],
        out_shape=[
            jax.ShapeDtypeStruct((rows, columns), jnp.float32),
            jax.ShapeDtypeStruct((rows // 128, 128), jnp.float32),
            jax.ShapeDtypeStruct((listed, 128), jnp.float32),
        ],
        scratch_shapes=[pltpu.VMEM((rows, 128), jnp.float32)],
        compiler_params=params(16),
        cost_estimate=pl.CostEstimate(
            flops=2 * rows * columns * width,
            bytes_accessed=2 * (rows + columns) * width + 4 * rows * columns,
            transcendentals=rows * columns,
        ),
        name="chunk_scores",
    )(*xs, y, u, *lses)


def merge_kernel(first_ref, second_ref, out_ref):
    out_ref[...] = log2_sum([first_ref[...], second_ref[...]])


def merge_call(first, second):
    return pl.pallas_call(
        merge_kernel,
        in_specs=[WHOLE, WHOLE],
        out_specs=WHOLE,
        out_shape=jax.ShapeDtypeStruct(first.shape, jnp.float32),
        compiler_params=params(1),
        cost_estimate=pl.CostEstimate(flops=8 * first.size, bytes_accessed=12 * first.size, transcendentals=0),
        name="merge_rows",
    )(first, second)


def weight_kernel(count, held, *refs):
    top_refs, (stat_ref, logw_ref, base_ref, most_ref) = refs[:count], refs[count:]
    at = 0
    for top_ref in top_refs:
        for r in range(top_ref.shape[0]):
            base_ref[pl.ds(canonical(held, at), 1), :] = top_ref[r:r + 1, :]
            at += 1
    base = base_ref[...] + logw_ref[...] * LOG2E
    bound = base - stat_ref[...]
    most = jnp.max(jnp.max(bound, axis=0, keepdims=True), axis=1, keepdims=True)
    base_ref[...] = base - most
    most_ref[...] = jnp.broadcast_to(most, most_ref.shape)


def weight_call(held, tops, stat, logw):
    shape = jax.ShapeDtypeStruct(stat.shape, jnp.float32)
    return pl.pallas_call(
        functools.partial(weight_kernel, len(tops), held),
        in_specs=[WHOLE] * (len(tops) + 2),
        out_specs=[WHOLE, WHOLE],
        out_shape=[shape, shape],
        compiler_params=params(1),
        cost_estimate=pl.CostEstimate(flops=8 * stat.size, bytes_accessed=16 * stat.size, transcendentals=0),
        name="row_weights",
    )(*tops, stat, logw)


def column_kernel(scale, counts, held, *refs):
    refs = list(refs)
    stat_refs, e_refs, x_refs = [[refs.pop(0) for _ in range(n)] for n in counts]
    base_ref, most_ref, logw_ref, u_ref, y_ref, out_ref, total_ref, v_ref, wide_ref, score_ref = refs
    columns = u_ref.shape[1]
    stats = [r[...] for r in stat_refs]
    top = functools.reduce(jnp.maximum, stats)
    share = functools.reduce(jnp.add, [jnp.exp2(p - top) for p in stats])
    most = most_ref[0:1, :]

    count = base_ref.shape[0]
    part_row = lax.broadcasted_iota(jnp.int32, (4 * count, 128 * count), 0)
    lane_row = lax.broadcasted_iota(jnp.int32, (4 * count, 128 * count), 1) // 128
    pattern = jnp.where(part_row % count == lane_row, 1.0, 0.0).astype(jnp.bfloat16)

    def spread(rows):
        parts = []
        for _ in range(3):
            parts.append(rows.astype(jnp.bfloat16).astype(jnp.float32))
            rows = rows - parts[-1]
        parts = jnp.concatenate(parts + [jnp.zeros_like(rows)], axis=0).astype(jnp.bfloat16)
        laid = lax.dot_general(parts, pattern, (((0,), (0,)), ((), ())), preferred_element_type=jnp.float32)
        for r in range(count):
            wide_ref[r * 128:(r + 1) * 128, :] = laid[:, r * 128:(r + 1) * 128]

    spread(jnp.exp2(base_ref[...] - top) / share)
    total_ref[...] = top + jnp.log2(share)
    starts = [sum(e.shape[0] for e in e_refs[:i]) // 128 for i in range(len(e_refs))]
    places = []
    for e_ref, start in zip(e_refs, starts):
        for r in range(0, e_ref.shape[0], 8):
            if r % 128 == 0:
                from_row = canonical(held, start + r // 128) * 128
            places.append((e_ref, r, pl.ds(pl.multiple_of(from_row + r % 128, 8), 8)))

    strips = columns // 128
    sums = [[] for _ in range(strips)]
    for first in range(0, len(places), 2):
        group = places[first:first + 2]
        weights = [wide_ref[at, :] for _, _, at in group]
        for s, part in enumerate(sums):
            terms = [e_ref[r:r + 8, s * 128:(s + 1) * 128] * a for (e_ref, r, _), a in zip(group, weights)]
            part[:] = [tree_sum(part + [tree_sum(terms)])]
    rows = jnp.concatenate([jnp.sum(part[0], axis=0, keepdims=True) for part in sums], axis=0)
    shifts = jnp.concatenate([u_ref[:, s * 128:(s + 1) * 128] for s in range(strips)], axis=0)
    out_ref[...] = jnp.log2(rows) + (most - shifts)
    least = jnp.min(rows, axis=0, keepdims=True)

    @pl.when(jnp.logical_not(jnp.min(least) > SMALL))
    def _():
        v_ref[...] = logw_ref[...] * LOG2E - total_ref[...]
        spread(v_ref[...])

        @pl.loop(0, columns // 128)
        def _(strip):
            y = y_ref[pl.ds(pl.multiple_of(strip * 128, 128), 128), :]
            at = 0
            for x_ref in x_refs:
                span = slice(at, at + x_ref.shape[0])
                v = wide_ref[pl.ds(pl.multiple_of(canonical(held, at // 128) * 128, 128), 128), :]
                score_ref[span, :] = scaled_product(x_ref[...], y, scale) + v
                at += x_ref.shape[0]
            top = jnp.max(score_ref[...], axis=0, keepdims=True)
            row = jnp.sum(jnp.exp2(score_ref[...] - top), axis=0, keepdims=True)
            out_ref[pl.ds(strip, 1), :] = top + jnp.log2(row)


def column_call(held, stats, exps, pieces, base, most, logw, u, y):
    first = stats[0]
    columns, width = y.shape
    rows = 128 * first.shape[0]
    lists = [stats, exps, pieces]
    scale = 2.0 * LOG2E / (width * smoothing)
    return pl.pallas_call(
        functools.partial(column_kernel, scale, [len(part) for part in lists], held),
        in_specs=[WHOLE] * (sum(len(part) for part in lists) + 5),
        out_specs=[WHOLE, WHOLE],
        out_shape=[
            jax.ShapeDtypeStruct((columns // 128, 128), jnp.float32),
            jax.ShapeDtypeStruct(first.shape, jnp.float32),
        ],
        scratch_shapes=[
            pltpu.VMEM(first.shape, jnp.float32),
            pltpu.VMEM((rows, 128), jnp.float32),
            pltpu.VMEM((rows, 128), jnp.float32),
        ],
        compiler_params=params(20),
        cost_estimate=pl.CostEstimate(
            flops=2 * rows * columns,
            bytes_accessed=4 * rows * columns,
            transcendentals=0,
        ),
        name="column_lse",
    )(*stats, *exps, *pieces, base, most, logw, u, y)


def pot_kernel(inverse, held, parts, total_ref, *refs):
    x_refs, pot_ref = refs[:parts], refs[parts]
    squares = []
    for x_ref in x_refs:
        squares.append(folded(jnp.square(x_ref[...].astype(jnp.float32))))
    squares = jnp.concatenate(squares, axis=0)
    for h in range(squares.shape[0] // 128):
        norm = jnp.sum(jnp.transpose(squares[h * 128:(h + 1) * 128]), axis=0, keepdims=True)
        row = pl.ds(canonical(held, h), 1)
        pot_ref[row, :] = norm * inverse - total_ref[row, :] * LN2


def pot_call(held, total, pieces, inverse):
    return pl.pallas_call(
        functools.partial(pot_kernel, inverse, held, len(pieces)),
        in_specs=[WHOLE] * (1 + len(pieces)),
        out_specs=WHOLE,
        out_shape=jax.ShapeDtypeStruct(total.shape, jnp.float32),
        compiler_params=params(12),
        cost_estimate=pl.CostEstimate(
            flops=2 * sum(x.size for x in pieces),
            bytes_accessed=2 * sum(x.size for x in pieces),
            transcendentals=0,
        ),
        name="treated_pot",
    )(total, *pieces)


def body(chips, treated_emb, control_emb, control_pot, control_logw, treated_logw):
    width = control_emb.shape[1]
    inverse = 1.0 / (width * smoothing)
    control_sq = jnp.sum(jnp.square(control_emb.astype(jnp.float32)), axis=1) * inverse
    u = ((control_pot + control_logw - control_sq) * LOG2E)[None, :]
    logw = treated_logw.reshape(-1, 128)
    rows = treated_emb.shape[0]
    ring = chips == 4 and rows == 128

    def moved(value, target):
        perm = [(z * 2 + c, target(z, c)) for z in range(chips) for c in range(2)]
        return lax.ppermute(value, "control", perm)

    def swapped(value):
        return moved(value, lambda z, c: z * 2 + 1 - c)

    def shifted(value, shift):
        return moved(value, lambda z, c: (z + shift) % chips * 2 + c)

    if ring:
        held = (chips, ((0, 0), (0, 1), (1, 0), (3, 0), (1, 1), (3, 1), (2, 0), (2, 1)))
        x0 = treated_emb
        x1 = shifted(x0, 1)
        p0 = swapped(x0)
        behind, u = lax.optimization_barrier((x0, u))
        x3 = shifted(behind, 3)
        e0, top0, lse0 = chunk_call([x0, p0], control_emb, u)
        x1, lse0 = lax.optimization_barrier((x1, lse0))
        x2 = shifted(x1, 1)
        x1, x3 = lax.optimization_barrier((x1, x3))
        e1, top1, lse1 = chunk_call([x1, x3], control_emb, u)
        x1, x3, lse1 = lax.optimization_barrier((x1, x3, lse1))
        p1 = swapped(x1)
        p3 = swapped(x3)
        p1, p3, x2 = lax.optimization_barrier((p1, p3, x2))
        p2 = swapped(x2)
        e2, top2, lse2 = chunk_call([p1, p3], control_emb, u)
        p2, lse2 = lax.optimization_barrier((p2, lse2))
        e3, top3, stats = chunk_call([x2, p2], control_emb, u, held, [lse0, lse1, lse2])
        exps, tops = [e0, e1, e2, e3], [top0, top1, top2, top3]
        pieces = [x0, p0, x1, x3, p1, p3, x2, p2]
        chip_stats = merge_call(stats, swapped(stats))
        stats = [chip_stats]
        for flip in (1, 2, 3):
            stats.append(moved(chip_stats, lambda z, c: (z ^ flip) * 2 + c))
    else:
        held = None
        block = lax.all_gather(treated_emb, "control", axis=0, tiled=True)
        pieces = [block[i:i + 128] for i in range(0, block.shape[0], 128)]
        exps, tops, lses = [], [], []
        for k in range(0, len(pieces), 2):
            e, top, lse = chunk_call(pieces[k:k + 2], control_emb, u)
            exps.append(e)
            tops.append(top)
            lses.append(lse)
        gathered = lax.all_gather(jnp.concatenate(lses, axis=0), "control")
        top = jnp.max(gathered, axis=0)
        stats = [top + jnp.log2(jnp.sum(jnp.exp2(gathered - top[None]), axis=0))]

    if ring:
        pieces = list(lax.optimization_barrier((tuple(pieces), stats[-1]))[0])
    base, most = weight_call(held, tops, stats[0], logw)
    column, total = column_call(held, stats, exps, pieces, base, most, logw, u, control_emb)
    treated_pot = pot_call(held, total, pieces, inverse).reshape(-1)

    size = lax.axis_size("treated")
    if size == 4:
        parts = [column]
        for flip in (1, 2, 3):
            parts.append(lax.ppermute(column, "treated", [(s, s ^ flip) for s in range(size)]))
    else:
        gathered = lax.all_gather(column, "treated")
        parts = [gathered[s] for s in range(size)]
    column_lse = log2_sum(parts).reshape(-1) * LN2 - control_sq
    return (treated_pot, column_lse)


def solution(mesh):
    placed = (
        P(("treated", "control"), None),
        P("control", None),
        P("control"),
        P("control"),
        P("treated"),
    )
    return jax.shard_map(
        functools.partial(body, mesh.shape["control"] // 2),
        mesh=mesh,
        in_specs=placed,
        out_specs=(P("treated"), P("control")),
        check_vma=False,
    )
```

```python
import functools

import jax
import jax.numpy as jnp
from jax import lax
from jax.experimental import pallas as pl
from jax.experimental.pallas import tpu as pltpu
from jax.sharding import PartitionSpec as P

smoothing = 0.1
LOG2E = 1.4426950408889634
LN2 = 0.6931471805599453
LARGE = 2.0**30
SMALL = 2.0**-50
MIB = 1024 * 1024
NT_DIMS = (((1,), (1,)), ((), ()))
WHOLE = pl.BlockSpec(memory_space=pltpu.VMEM)


def params(limit):
    return pltpu.CompilerParams(vmem_limit_bytes=limit * MIB)


def canonical(held, piece):
    if held is None:
        return piece
    chips, places = held
    me = lax.axis_index("control")
    shift, flip = places[piece]
    return (me // 2 + chips - shift) % chips * 2 + (me % 2 + flip) % 2


def log2_sum(parts):
    top = functools.reduce(jnp.maximum, parts)
    return top + jnp.log2(functools.reduce(jnp.add, [jnp.exp2(p - top) for p in parts]))


def turned(column):
    return jnp.transpose(jnp.broadcast_to(column, (128, 128)))[0:1, :]


def tree_sum(parts):
    while len(parts) > 1:
        parts = [functools.reduce(jnp.add, parts[i:i + 2]) for i in range(0, len(parts), 2)]
    return parts[0]


def folded(wide):
    return functools.reduce(jnp.add, [wide[:, j:j + 128] for j in range(0, wide.shape[1], 128)])


def scaled_product(x, y, scale):
    return lax.dot_general(x, y, NT_DIMS, preferred_element_type=jnp.float32) * scale


def chunk_kernel(scale, parts, earlier, held, *refs):
    x_refs, refs = refs[:parts], refs[parts:]
    y_ref, u_ref, refs = refs[0], refs[1], refs[2:]
    lse_refs, (e_ref, top_ref, lse_ref, wide_ref) = refs[:earlier], refs[earlier:]
    columns = y_ref.shape[0]
    x = jnp.concatenate([r[...] for r in x_refs], axis=0)
    rows = x.shape[0]
    tile = 256
    before = [r[h:h + 1, :] for r in lse_refs for h in range(r.shape[0])]

    def emit(top, total):
        own, sums = [], []
        for h in range(0, rows, 128):
            shift = turned(top[h:h + 128])
            row = jnp.sum(jnp.transpose(total[h:h + 128]), axis=0, keepdims=True)
            top_ref[h // 128:h // 128 + 1, :] = shift
            own.append(shift + jnp.log2(row))
            sums.append(row)
        for h, row in enumerate(before + own):
            if earlier:
                lse_ref[pl.ds(canonical(held, h), 1), :] = row
            else:
                lse_ref[h:h + 1, :] = row
        return functools.reduce(jnp.maximum, sums)

    top, total = None, None
    for j in range(0, columns, tile):
        t = scaled_product(x, y_ref[j:j + tile, :], scale) + u_ref[:, j:j + tile]
        if top is None:
            top = jnp.max(t, axis=1, keepdims=True)
        e = jnp.exp2(t - top)
        e_ref[:, j:j + tile] = e
        total = folded(e) if total is None else total + folded(e)
    largest = emit(top, total)

    @pl.when(jnp.logical_not(jnp.max(largest) < LARGE))
    def _():
        def scores(j):
            place = pl.ds(pl.multiple_of(j * tile, tile), tile)
            return place, scaled_product(x, y_ref[place, :], scale) + u_ref[:, place]

        wide_ref[...] = jnp.full_like(wide_ref, -jnp.inf)

        @pl.loop(0, columns // tile)
        def _(j):
            wide_ref[...] = jnp.maximum(wide_ref[...], jnp.max(scores(j)[1], axis=1, keepdims=True))

        top = wide_ref[:, 0:1]
        wide_ref[...] = jnp.zeros_like(wide_ref)

        @pl.loop(0, columns // tile)
        def _(j):
            place, t = scores(j)
            e = jnp.exp2(t - top)
            e_ref[:, place] = e
            wide_ref[...] += folded(e)

        emit(top, wide_ref[...])


def chunk_call(xs, y, u, held=None, lses=(), hidden=False):
    parts = len(xs)
    width = xs[0].shape[1]
    columns = y.shape[0]
    rows = sum(x.shape[0] for x in xs)
    scale = 2.0 * LOG2E / (width * smoothing)
    listed = rows // 128 + sum(a.shape[0] for a in lses)
    return pl.pallas_call(
        functools.partial(chunk_kernel, scale, parts, len(lses), held),
        in_specs=[WHOLE] * (parts + 2 + len(lses)),
        out_specs=[WHOLE, WHOLE, WHOLE],
        out_shape=[
            jax.ShapeDtypeStruct((rows, columns), jnp.float32),
            jax.ShapeDtypeStruct((rows // 128, 128), jnp.float32),
            jax.ShapeDtypeStruct((listed, 128), jnp.float32),
        ],
        scratch_shapes=[pltpu.VMEM((rows, 128), jnp.float32)],
        compiler_params=params(16),
        cost_estimate=pl.CostEstimate(
            flops=0 if hidden else 2 * rows * columns * width,
            bytes_accessed=0 if hidden else 2 * (rows + columns) * width + 4 * rows * columns,
            transcendentals=0 if hidden else rows * columns,
        ),
        name="chunk_scores",
    )(*xs, y, u, *lses)


def halves_kernel(count, *refs):
    for x_ref, first_ref, second_ref in zip(refs[:count], refs[count::2], refs[count + 1::2]):
        half = first_ref.shape[0]
        first_ref[...] = x_ref[:half, :]
        second_ref[...] = x_ref[half:, :]


def halves_call(xs):
    half = jax.ShapeDtypeStruct((xs[0].shape[0] // 2, xs[0].shape[1]), xs[0].dtype)
    return pl.pallas_call(
        functools.partial(halves_kernel, len(xs)),
        in_specs=[WHOLE] * len(xs),
        out_specs=[WHOLE] * (2 * len(xs)),
        out_shape=[half] * (2 * len(xs)),
        compiler_params=params(4),
        cost_estimate=pl.CostEstimate(flops=0, bytes_accessed=0, transcendentals=0),
        name="halves",
    )(*xs)


def merge_kernel(first_ref, second_ref, out_ref):
    out_ref[...] = log2_sum([first_ref[...], second_ref[...]])


def merge_call(first, second):
    return pl.pallas_call(
        merge_kernel,
        in_specs=[WHOLE, WHOLE],
        out_specs=WHOLE,
        out_shape=jax.ShapeDtypeStruct(first.shape, jnp.float32),
        compiler_params=params(1),
        cost_estimate=pl.CostEstimate(flops=8 * first.size, bytes_accessed=12 * first.size, transcendentals=0),
        name="merge_rows",
    )(first, second)


def weight_kernel(count, held, *refs):
    top_refs, (stat_ref, logw_ref, base_ref, most_ref) = refs[:count], refs[count:]
    at = 0
    for top_ref in top_refs:
        for r in range(top_ref.shape[0]):
            base_ref[pl.ds(canonical(held, at), 1), :] = top_ref[r:r + 1, :]
            at += 1
    base = base_ref[...] + logw_ref[...] * LOG2E
    bound = base - stat_ref[...]
    most = jnp.max(jnp.max(bound, axis=0, keepdims=True), axis=1, keepdims=True)
    base_ref[...] = base - most
    most_ref[...] = jnp.broadcast_to(most, most_ref.shape)


def weight_call(held, tops, stat, logw):
    shape = jax.ShapeDtypeStruct(stat.shape, jnp.float32)
    return pl.pallas_call(
        functools.partial(weight_kernel, len(tops), held),
        in_specs=[WHOLE] * (len(tops) + 2),
        out_specs=[WHOLE, WHOLE],
        out_shape=[shape, shape],
        compiler_params=params(1),
        cost_estimate=pl.CostEstimate(flops=8 * stat.size, bytes_accessed=16 * stat.size, transcendentals=0),
        name="row_weights",
    )(*tops, stat, logw)


def column_kernel(scale, counts, held, *refs):
    refs = list(refs)
    stat_refs, e_refs, x_refs = [[refs.pop(0) for _ in range(n)] for n in counts]
    base_ref, most_ref, logw_ref, u_ref, y_ref, out_ref, total_ref, v_ref, wide_ref, score_ref = refs
    columns = u_ref.shape[1]
    stats = [r[...] for r in stat_refs]
    top = functools.reduce(jnp.maximum, stats)
    share = functools.reduce(jnp.add, [jnp.exp2(p - top) for p in stats])
    most = most_ref[0:1, :]

    count = base_ref.shape[0]
    part_row = lax.broadcasted_iota(jnp.int32, (4 * count, 128 * count), 0)
    lane_row = lax.broadcasted_iota(jnp.int32, (4 * count, 128 * count), 1) // 128
    pattern = jnp.where(part_row % count == lane_row, 1.0, 0.0).astype(jnp.bfloat16)

    def spread(rows):
        parts = []
        for _ in range(3):
            parts.append(rows.astype(jnp.bfloat16).astype(jnp.float32))
            rows = rows - parts[-1]
        parts = jnp.concatenate(parts + [jnp.zeros_like(rows)], axis=0).astype(jnp.bfloat16)
        laid = lax.dot_general(parts, pattern, (((0,), (0,)), ((), ())), preferred_element_type=jnp.float32)
        for r in range(count):
            wide_ref[r * 128:(r + 1) * 128, :] = laid[:, r * 128:(r + 1) * 128]

    spread(jnp.exp2(base_ref[...] - top) / share)
    total_ref[...] = top + jnp.log2(share)
    starts = [sum(e.shape[0] for e in e_refs[:i]) // 128 for i in range(len(e_refs))]
    places = []
    for e_ref, start in zip(e_refs, starts):
        for r in range(0, e_ref.shape[0], 8):
            if r % 128 == 0:
                from_row = canonical(held, start + r // 128) * 128
            places.append((e_ref, r, pl.ds(pl.multiple_of(from_row + r % 128, 8), 8)))

    strips = columns // 128
    sums = [[] for _ in range(strips)]
    for first in range(0, len(places), 2):
        group = places[first:first + 2]
        weights = [wide_ref[at, :] for _, _, at in group]
        for s, part in enumerate(sums):
            terms = [e_ref[r:r + 8, s * 128:(s + 1) * 128] * a for (e_ref, r, _), a in zip(group, weights)]
            part[:] = [tree_sum(part + [tree_sum(terms)])]
    rows = jnp.concatenate([jnp.sum(part[0], axis=0, keepdims=True) for part in sums], axis=0)
    shifts = jnp.concatenate([u_ref[:, s * 128:(s + 1) * 128] for s in range(strips)], axis=0)
    out_ref[...] = jnp.log2(rows) + (most - shifts)
    least = jnp.min(rows, axis=0, keepdims=True)

    @pl.when(jnp.logical_not(jnp.min(least) > SMALL))
    def _():
        v_ref[...] = logw_ref[...] * LOG2E - total_ref[...]
        spread(v_ref[...])

        @pl.loop(0, columns // 128)
        def _(strip):
            y = y_ref[pl.ds(pl.multiple_of(strip * 128, 128), 128), :]
            at = 0
            for x_ref in x_refs:
                span = slice(at, at + x_ref.shape[0])
                from_row = canonical(held, at // 128) * 128 + at % 128
                v = wide_ref[pl.ds(pl.multiple_of(from_row, 8), x_ref.shape[0]), :]
                score_ref[span, :] = scaled_product(x_ref[...], y, scale) + v
                at += x_ref.shape[0]
            top = jnp.max(score_ref[...], axis=0, keepdims=True)
            row = jnp.sum(jnp.exp2(score_ref[...] - top), axis=0, keepdims=True)
            out_ref[pl.ds(strip, 1), :] = top + jnp.log2(row)


def column_call(held, stats, exps, pieces, base, most, logw, u, y):
    first = stats[0]
    columns, width = y.shape
    rows = 128 * first.shape[0]
    lists = [stats, exps, pieces]
    scale = 2.0 * LOG2E / (width * smoothing)
    return pl.pallas_call(
        functools.partial(column_kernel, scale, [len(part) for part in lists], held),
        in_specs=[WHOLE] * (sum(len(part) for part in lists) + 5),
        out_specs=[WHOLE, WHOLE],
        out_shape=[
            jax.ShapeDtypeStruct((columns // 128, 128), jnp.float32),
            jax.ShapeDtypeStruct(first.shape, jnp.float32),
        ],
        scratch_shapes=[
            pltpu.VMEM(first.shape, jnp.float32),
            pltpu.VMEM((rows, 128), jnp.float32),
            pltpu.VMEM((rows, 128), jnp.float32),
        ],
        compiler_params=params(20),
        cost_estimate=pl.CostEstimate(
            flops=2 * rows * columns,
            bytes_accessed=4 * rows * columns,
            transcendentals=0,
        ),
        name="column_lse",
    )(*stats, *exps, *pieces, base, most, logw, u, y)


def pot_kernel(inverse, held, parts, total_ref, *refs):
    x_refs, pot_ref = refs[:parts], refs[parts]
    squares = []
    for x_ref in x_refs:
        squares.append(folded(jnp.square(x_ref[...].astype(jnp.float32))))
    squares = jnp.concatenate(squares, axis=0)
    for h in range(squares.shape[0] // 128):
        norm = jnp.sum(jnp.transpose(squares[h * 128:(h + 1) * 128]), axis=0, keepdims=True)
        row = pl.ds(canonical(held, h), 1)
        pot_ref[row, :] = norm * inverse - total_ref[row, :] * LN2


def pot_call(held, total, pieces, inverse):
    return pl.pallas_call(
        functools.partial(pot_kernel, inverse, held, len(pieces)),
        in_specs=[WHOLE] * (1 + len(pieces)),
        out_specs=WHOLE,
        out_shape=jax.ShapeDtypeStruct(total.shape, jnp.float32),
        compiler_params=params(12),
        cost_estimate=pl.CostEstimate(
            flops=2 * sum(x.size for x in pieces),
            bytes_accessed=2 * sum(x.size for x in pieces),
            transcendentals=0,
        ),
        name="treated_pot",
    )(total, *pieces)


def body(chips, treated_emb, control_emb, control_pot, control_logw, treated_logw):
    width = control_emb.shape[1]
    inverse = 1.0 / (width * smoothing)
    control_sq = jnp.sum(jnp.square(control_emb.astype(jnp.float32)), axis=1) * inverse
    u = ((control_pot + control_logw - control_sq) * LOG2E)[None, :]
    logw = treated_logw.reshape(-1, 128)
    rows = treated_emb.shape[0]
    ring = chips == 4 and rows == 128

    def moved(value, target):
        perm = [(z * 2 + c, target(z, c)) for z in range(chips) for c in range(2)]
        return lax.ppermute(value, "control", perm)

    def swapped(value):
        return moved(value, lambda z, c: z * 2 + 1 - c)

    def shifted(value, shift):
        return moved(value, lambda z, c: (z + shift) % chips * 2 + c)

    if ring:
        held = (chips, ((0, 0), (0, 1), (1, 0), (1, 1), (3, 0), (3, 1), (2, 0), (2, 1)))
        x0 = treated_emb
        x1 = shifted(x0, 1)
        p0 = swapped(x0)
        behind, u = lax.optimization_barrier((x0, u))
        x3 = shifted(behind, 3)
        e0, top0, lse0 = chunk_call([x0, p0], control_emb, u)
        x1, lse0 = lax.optimization_barrier((x1, lse0))
        x2 = shifted(x1, 1)
        p1 = [swapped(part) for part in halves_call([x1])]
        e1, top1, lse1 = chunk_call([x1, *p1], control_emb, u, hidden=True)
        x3, lse1 = lax.optimization_barrier((x3, lse1))
        p3 = [swapped(part) for part in halves_call([x3])]
        e2, top2, lse2 = chunk_call([x3, *p3], control_emb, u, hidden=True)
        x2, lse2 = lax.optimization_barrier((x2, lse2))
        p2 = swapped(x2)
        e3, top3, stats = chunk_call([x2, p2], control_emb, u, held, [lse0, lse1, lse2])
        exps, tops = [e0, e1, e2, e3], [top0, top1, top2, top3]
        pieces = [x0, p0, x1, *p1, x3, *p3, x2, p2]
        chip_stats = merge_call(stats, swapped(stats))
        stats = [chip_stats]
        for flip in (1, 2, 3):
            stats.append(moved(chip_stats, lambda z, c: (z ^ flip) * 2 + c))
    else:
        held = None
        block = lax.all_gather(treated_emb, "control", axis=0, tiled=True)
        pieces = [block[i:i + 128] for i in range(0, block.shape[0], 128)]
        exps, tops, lses = [], [], []
        for k in range(0, len(pieces), 2):
            e, top, lse = chunk_call(pieces[k:k + 2], control_emb, u)
            exps.append(e)
            tops.append(top)
            lses.append(lse)
        gathered = lax.all_gather(jnp.concatenate(lses, axis=0), "control")
        top = jnp.max(gathered, axis=0)
        stats = [top + jnp.log2(jnp.sum(jnp.exp2(gathered - top[None]), axis=0))]

    if ring:
        pieces = list(lax.optimization_barrier((tuple(pieces), stats[-1]))[0])
    base, most = weight_call(held, tops, stats[0], logw)
    column, total = column_call(held, stats, exps, pieces, base, most, logw, u, control_emb)
    treated_pot = pot_call(held, total, pieces, inverse).reshape(-1)

    size = lax.axis_size("treated")
    if size == 4:
        parts = [column]
        for flip in (1, 2, 3):
            parts.append(lax.ppermute(column, "treated", [(s, s ^ flip) for s in range(size)]))
    else:
        gathered = lax.all_gather(column, "treated")
        parts = [gathered[s] for s in range(size)]
    column_lse = log2_sum(parts).reshape(-1) * LN2 - control_sq
    return (treated_pot, column_lse)


def solution(mesh):
    placed = (
        P(("treated", "control"), None),
        P("control", None),
        P("control"),
        P("control"),
        P("treated"),
    )
    return jax.shard_map(
        functools.partial(body, mesh.shape["control"] // 2),
        mesh=mesh,
        in_specs=placed,
        out_specs=(P("treated"), P("control")),
        check_vma=False,
    )
```

```python
import functools

import jax
import jax.numpy as jnp
from jax import lax
from jax.experimental import pallas as pl
from jax.experimental.pallas import tpu as pltpu
from jax.sharding import PartitionSpec as P

smoothing = 0.1
LOG2E = 1.4426950408889634
LN2 = 0.6931471805599453
LARGE = 2.0**30
SMALL = 2.0**-50
MIB = 1024 * 1024
NT_DIMS = (((1,), (1,)), ((), ()))
WHOLE = pl.BlockSpec(memory_space=pltpu.VMEM)


def params(limit):
    return pltpu.CompilerParams(vmem_limit_bytes=limit * MIB)


def canonical(held, piece):
    if held is None:
        return piece
    chips, places = held
    me = lax.axis_index("control")
    shift, flip = places[piece]
    return (me // 2 + chips - shift) % chips * 2 + (me % 2 + flip) % 2


def log2_sum(parts):
    top = functools.reduce(jnp.maximum, parts)
    return top + jnp.log2(functools.reduce(jnp.add, [jnp.exp2(p - top) for p in parts]))


def turned(column):
    return jnp.transpose(jnp.broadcast_to(column, (128, 128)))[0:1, :]


def tree_sum(parts):
    while len(parts) > 1:
        parts = [functools.reduce(jnp.add, parts[i:i + 2]) for i in range(0, len(parts), 2)]
    return parts[0]


def folded(wide):
    return functools.reduce(jnp.add, [wide[:, j:j + 128] for j in range(0, wide.shape[1], 128)])


def scaled_product(x, y, scale):
    return lax.dot_general(x, y, NT_DIMS, preferred_element_type=jnp.float32) * scale


def chunk_kernel(scale, parts, earlier, held, *refs):
    x_refs, refs = refs[:parts], refs[parts:]
    y_ref, u_ref, refs = refs[0], refs[1], refs[2:]
    lse_refs, (e_ref, top_ref, lse_ref, wide_ref) = refs[:earlier], refs[earlier:]
    columns = y_ref.shape[0]
    x = jnp.concatenate([r[...] for r in x_refs], axis=0)
    rows = x.shape[0]
    tile = 256
    before = [r[h:h + 1, :] for r in lse_refs for h in range(r.shape[0])]

    def emit(top, total):
        own, sums = [], []
        for h in range(0, rows, 128):
            shift = turned(top[h:h + 128])
            row = jnp.sum(jnp.transpose(total[h:h + 128]), axis=0, keepdims=True)
            top_ref[h // 128:h // 128 + 1, :] = shift
            own.append(shift + jnp.log2(row))
            sums.append(row)
        for h, row in enumerate(before + own):
            if earlier:
                lse_ref[pl.ds(canonical(held, h), 1), :] = row
            else:
                lse_ref[h:h + 1, :] = row
        return functools.reduce(jnp.maximum, sums)

    top, total = None, None
    for j in range(0, columns, tile):
        t = scaled_product(x, y_ref[j:j + tile, :], scale) + u_ref[:, j:j + tile]
        if top is None:
            top = jnp.max(t, axis=1, keepdims=True)
        e = jnp.exp2(t - top)
        e_ref[:, j:j + tile] = e
        total = folded(e) if total is None else total + folded(e)
    largest = emit(top, total)

    @pl.when(jnp.logical_not(jnp.max(largest) < LARGE))
    def _():
        def scores(j):
            place = pl.ds(pl.multiple_of(j * tile, tile), tile)
            return place, scaled_product(x, y_ref[place, :], scale) + u_ref[:, place]

        wide_ref[...] = jnp.full_like(wide_ref, -jnp.inf)

        @pl.loop(0, columns // tile)
        def _(j):
            wide_ref[...] = jnp.maximum(wide_ref[...], jnp.max(scores(j)[1], axis=1, keepdims=True))

        top = wide_ref[:, 0:1]
        wide_ref[...] = jnp.zeros_like(wide_ref)

        @pl.loop(0, columns // tile)
        def _(j):
            place, t = scores(j)
            e = jnp.exp2(t - top)
            e_ref[:, place] = e
            wide_ref[...] += folded(e)

        emit(top, wide_ref[...])


def chunk_call(xs, y, u, held=None, lses=(), hidden=False):
    parts = len(xs)
    width = xs[0].shape[1]
    columns = y.shape[0]
    rows = sum(x.shape[0] for x in xs)
    scale = 2.0 * LOG2E / (width * smoothing)
    listed = rows // 128 + sum(a.shape[0] for a in lses)
    return pl.pallas_call(
        functools.partial(chunk_kernel, scale, parts, len(lses), held),
        in_specs=[WHOLE] * (parts + 2 + len(lses)),
        out_specs=[WHOLE, WHOLE, WHOLE],
        out_shape=[
            jax.ShapeDtypeStruct((rows, columns), jnp.float32),
            jax.ShapeDtypeStruct((rows // 128, 128), jnp.float32),
            jax.ShapeDtypeStruct((listed, 128), jnp.float32),
        ],
        scratch_shapes=[pltpu.VMEM((rows, 128), jnp.float32)],
        compiler_params=params(16),
        cost_estimate=pl.CostEstimate(
            flops=0 if hidden else 2 * rows * columns * width,
            bytes_accessed=0 if hidden else 2 * (rows + columns) * width + 4 * rows * columns,
            transcendentals=0 if hidden else rows * columns,
        ),
        name="chunk_scores",
    )(*xs, y, u, *lses)


def halves_kernel(count, *refs):
    for x_ref, first_ref, second_ref in zip(refs[:count], refs[count::2], refs[count + 1::2]):
        half = first_ref.shape[0]
        first_ref[...] = x_ref[:half, :]
        second_ref[...] = x_ref[half:, :]


def halves_call(xs):
    half = jax.ShapeDtypeStruct((xs[0].shape[0] // 2, xs[0].shape[1]), xs[0].dtype)
    return pl.pallas_call(
        functools.partial(halves_kernel, len(xs)),
        in_specs=[WHOLE] * len(xs),
        out_specs=[WHOLE] * (2 * len(xs)),
        out_shape=[half] * (2 * len(xs)),
        compiler_params=params(4),
        cost_estimate=pl.CostEstimate(flops=0, bytes_accessed=0, transcendentals=0),
        name="halves",
    )(*xs)


def merge_kernel(first_ref, second_ref, out_ref):
    out_ref[...] = log2_sum([first_ref[...], second_ref[...]])


def merge_call(first, second):
    return pl.pallas_call(
        merge_kernel,
        in_specs=[WHOLE, WHOLE],
        out_specs=WHOLE,
        out_shape=jax.ShapeDtypeStruct(first.shape, jnp.float32),
        compiler_params=params(1),
        cost_estimate=pl.CostEstimate(flops=8 * first.size, bytes_accessed=12 * first.size, transcendentals=0),
        name="merge_rows",
    )(first, second)


def weight_kernel(count, held, *refs):
    top_refs, (stat_ref, logw_ref, base_ref, most_ref) = refs[:count], refs[count:]
    at = 0
    for top_ref in top_refs:
        for r in range(top_ref.shape[0]):
            base_ref[pl.ds(canonical(held, at), 1), :] = top_ref[r:r + 1, :]
            at += 1
    base = base_ref[...] + logw_ref[...] * LOG2E
    bound = base - stat_ref[...]
    most = jnp.max(jnp.max(bound, axis=0, keepdims=True), axis=1, keepdims=True)
    base_ref[...] = base - most
    most_ref[...] = jnp.broadcast_to(most, most_ref.shape)


def weight_call(held, tops, stat, logw):
    shape = jax.ShapeDtypeStruct(stat.shape, jnp.float32)
    return pl.pallas_call(
        functools.partial(weight_kernel, len(tops), held),
        in_specs=[WHOLE] * (len(tops) + 2),
        out_specs=[WHOLE, WHOLE],
        out_shape=[shape, shape],
        compiler_params=params(1),
        cost_estimate=pl.CostEstimate(flops=8 * stat.size, bytes_accessed=16 * stat.size, transcendentals=0),
        name="row_weights",
    )(*tops, stat, logw)


def column_kernel(scale, counts, held, *refs):
    refs = list(refs)
    stat_refs, e_refs, x_refs = [[refs.pop(0) for _ in range(n)] for n in counts]
    base_ref, most_ref, logw_ref, u_ref, y_ref, out_ref, total_ref, v_ref, wide_ref, score_ref = refs
    columns = u_ref.shape[1]
    stats = [r[...] for r in stat_refs]
    top = functools.reduce(jnp.maximum, stats)
    share = functools.reduce(jnp.add, [jnp.exp2(p - top) for p in stats])
    most = most_ref[0:1, :]

    count = base_ref.shape[0]
    part_row = lax.broadcasted_iota(jnp.int32, (4 * count, 128 * count), 0)
    lane_row = lax.broadcasted_iota(jnp.int32, (4 * count, 128 * count), 1) // 128
    pattern = jnp.where(part_row % count == lane_row, 1.0, 0.0).astype(jnp.bfloat16)

    def spread(rows):
        parts = []
        for _ in range(3):
            parts.append(rows.astype(jnp.bfloat16).astype(jnp.float32))
            rows = rows - parts[-1]
        parts = jnp.concatenate(parts + [jnp.zeros_like(rows)], axis=0).astype(jnp.bfloat16)
        laid = lax.dot_general(parts, pattern, (((0,), (0,)), ((), ())), preferred_element_type=jnp.float32)
        for r in range(count):
            wide_ref[r * 128:(r + 1) * 128, :] = laid[:, r * 128:(r + 1) * 128]

    spread(jnp.exp2(base_ref[...] - top) / share)
    total_ref[...] = top + jnp.log2(share)
    starts = [sum(e.shape[0] for e in e_refs[:i]) // 128 for i in range(len(e_refs))]
    places = []
    for e_ref, start in zip(e_refs, starts):
        for r in range(0, e_ref.shape[0], 8):
            if r % 128 == 0:
                from_row = canonical(held, start + r // 128) * 128
            places.append((e_ref, r, pl.ds(pl.multiple_of(from_row + r % 128, 8), 8)))

    strips = columns // 128
    sums = [[] for _ in range(strips)]
    for first in range(0, len(places), 2):
        group = places[first:first + 2]
        weights = [wide_ref[at, :] for _, _, at in group]
        for s, part in enumerate(sums):
            terms = [e_ref[r:r + 8, s * 128:(s + 1) * 128] * a for (e_ref, r, _), a in zip(group, weights)]
            part[:] = [tree_sum(part + [tree_sum(terms)])]
    rows = jnp.concatenate([jnp.sum(part[0], axis=0, keepdims=True) for part in sums], axis=0)
    shifts = jnp.concatenate([u_ref[:, s * 128:(s + 1) * 128] for s in range(strips)], axis=0)
    out_ref[...] = jnp.log2(rows) + (most - shifts)
    least = jnp.min(rows, axis=0, keepdims=True)

    @pl.when(jnp.logical_not(jnp.min(least) > SMALL))
    def _():
        v_ref[...] = logw_ref[...] * LOG2E - total_ref[...]
        spread(v_ref[...])

        @pl.loop(0, columns // 128)
        def _(strip):
            y = y_ref[pl.ds(pl.multiple_of(strip * 128, 128), 128), :]
            at = 0
            for x_ref in x_refs:
                span = slice(at, at + x_ref.shape[0])
                from_row = canonical(held, at // 128) * 128 + at % 128
                v = wide_ref[pl.ds(pl.multiple_of(from_row, 8), x_ref.shape[0]), :]
                score_ref[span, :] = scaled_product(x_ref[...], y, scale) + v
                at += x_ref.shape[0]
            top = jnp.max(score_ref[...], axis=0, keepdims=True)
            row = jnp.sum(jnp.exp2(score_ref[...] - top), axis=0, keepdims=True)
            out_ref[pl.ds(strip, 1), :] = top + jnp.log2(row)


def column_call(held, stats, exps, pieces, base, most, logw, u, y):
    first = stats[0]
    columns, width = y.shape
    rows = 128 * first.shape[0]
    lists = [stats, exps, pieces]
    scale = 2.0 * LOG2E / (width * smoothing)
    return pl.pallas_call(
        functools.partial(column_kernel, scale, [len(part) for part in lists], held),
        in_specs=[WHOLE] * (sum(len(part) for part in lists) + 5),
        out_specs=[WHOLE, WHOLE],
        out_shape=[
            jax.ShapeDtypeStruct((columns // 128, 128), jnp.float32),
            jax.ShapeDtypeStruct(first.shape, jnp.float32),
        ],
        scratch_shapes=[
            pltpu.VMEM(first.shape, jnp.float32),
            pltpu.VMEM((rows, 128), jnp.float32),
            pltpu.VMEM((rows, 128), jnp.float32),
        ],
        compiler_params=params(20),
        cost_estimate=pl.CostEstimate(
            flops=2 * rows * columns,
            bytes_accessed=4 * rows * columns,
            transcendentals=0,
        ),
        name="column_lse",
    )(*stats, *exps, *pieces, base, most, logw, u, y)


def pot_kernel(inverse, held, parts, total_ref, *refs):
    x_refs, pot_ref = refs[:parts], refs[parts]
    squares = []
    for x_ref in x_refs:
        squares.append(folded(jnp.square(x_ref[...].astype(jnp.float32))))
    squares = jnp.concatenate(squares, axis=0)
    for h in range(squares.shape[0] // 128):
        norm = jnp.sum(jnp.transpose(squares[h * 128:(h + 1) * 128]), axis=0, keepdims=True)
        row = pl.ds(canonical(held, h), 1)
        pot_ref[row, :] = norm * inverse - total_ref[row, :] * LN2


def pot_call(held, total, pieces, inverse):
    return pl.pallas_call(
        functools.partial(pot_kernel, inverse, held, len(pieces)),
        in_specs=[WHOLE] * (1 + len(pieces)),
        out_specs=WHOLE,
        out_shape=jax.ShapeDtypeStruct(total.shape, jnp.float32),
        compiler_params=params(12),
        cost_estimate=pl.CostEstimate(
            flops=2 * sum(x.size for x in pieces),
            bytes_accessed=2 * sum(x.size for x in pieces),
            transcendentals=0,
        ),
        name="treated_pot",
    )(total, *pieces)


def body(chips, treated_emb, control_emb, control_pot, control_logw, treated_logw):
    width = control_emb.shape[1]
    inverse = 1.0 / (width * smoothing)
    control_sq = jnp.sum(jnp.square(control_emb.astype(jnp.float32)), axis=1) * inverse
    u = ((control_pot + control_logw - control_sq) * LOG2E)[None, :]
    logw = treated_logw.reshape(-1, 128)
    rows = treated_emb.shape[0]
    ring = chips == 4 and rows == 128

    def moved(value, target):
        perm = [(z * 2 + c, target(z, c)) for z in range(chips) for c in range(2)]
        return lax.ppermute(value, "control", perm)

    def swapped(value):
        return moved(value, lambda z, c: z * 2 + 1 - c)

    def shifted(value, shift):
        return moved(value, lambda z, c: (z + shift) % chips * 2 + c)

    if ring:
        held = (chips, ((0, 0), (0, 1), (1, 0), (1, 1), (3, 0), (3, 1), (2, 0), (2, 1)))
        x0 = treated_emb
        x1 = shifted(x0, 1)
        behind, control_sq = lax.optimization_barrier((x0, control_sq))
        p0 = [swapped(part) for part in halves_call([behind])]
        behind, u = lax.optimization_barrier((x0, u))
        x3 = shifted(behind, 3)
        e0, top0, lse0 = chunk_call([x0, *p0], control_emb, u)
        x1, lse0 = lax.optimization_barrier((x1, lse0))
        x2 = shifted(x1, 1)
        p1 = [swapped(part) for part in halves_call([x1])]
        e1, top1, lse1 = chunk_call([x1, *p1], control_emb, u, hidden=True)
        x3, lse1 = lax.optimization_barrier((x3, lse1))
        p3 = [swapped(part) for part in halves_call([x3])]
        e2, top2, lse2 = chunk_call([x3, *p3], control_emb, u, hidden=True)
        x2, lse2 = lax.optimization_barrier((x2, lse2))
        p2 = swapped(x2)
        e3, top3, stats = chunk_call([x2, p2], control_emb, u, held, [lse0, lse1, lse2])
        exps, tops = [e0, e1, e2, e3], [top0, top1, top2, top3]
        pieces = [x0, *p0, x1, *p1, x3, *p3, x2, p2]
        chip_stats = merge_call(stats, swapped(stats))
        stats = [chip_stats]
        for flip in (1, 2, 3):
            stats.append(moved(chip_stats, lambda z, c: (z ^ flip) * 2 + c))
    else:
        held = None
        block = lax.all_gather(treated_emb, "control", axis=0, tiled=True)
        pieces = [block[i:i + 128] for i in range(0, block.shape[0], 128)]
        exps, tops, lses = [], [], []
        for k in range(0, len(pieces), 2):
            e, top, lse = chunk_call(pieces[k:k + 2], control_emb, u)
            exps.append(e)
            tops.append(top)
            lses.append(lse)
        gathered = lax.all_gather(jnp.concatenate(lses, axis=0), "control")
        top = jnp.max(gathered, axis=0)
        stats = [top + jnp.log2(jnp.sum(jnp.exp2(gathered - top[None]), axis=0))]

    if ring:
        pieces = list(lax.optimization_barrier((tuple(pieces), stats[-1]))[0])
    base, most = weight_call(held, tops, stats[0], logw)
    column, total = column_call(held, stats, exps, pieces, base, most, logw, u, control_emb)
    treated_pot = pot_call(held, total, pieces, inverse).reshape(-1)

    size = lax.axis_size("treated")
    if size == 4:
        parts = [column]
        for flip in (1, 2, 3):
            parts.append(lax.ppermute(column, "treated", [(s, s ^ flip) for s in range(size)]))
    else:
        gathered = lax.all_gather(column, "treated")
        parts = [gathered[s] for s in range(size)]
    column_lse = log2_sum(parts).reshape(-1) * LN2 - control_sq
    return (treated_pot, column_lse)


def solution(mesh):
    placed = (
        P(("treated", "control"), None),
        P("control", None),
        P("control"),
        P("control"),
        P("treated"),
    )
    return jax.shard_map(
        functools.partial(body, mesh.shape["control"] // 2),
        mesh=mesh,
        in_specs=placed,
        out_specs=(P("treated"), P("control")),
        check_vma=False,
    )
```

```python
import functools

import jax
import jax.numpy as jnp
from jax import lax
from jax.experimental import pallas as pl
from jax.experimental.pallas import tpu as pltpu
from jax.sharding import PartitionSpec as P

smoothing = 0.1
LOG2E = 1.4426950408889634
LN2 = 0.6931471805599453
LARGE = 2.0**30
SMALL = 2.0**-50
MIB = 1024 * 1024
NT_DIMS = (((1,), (1,)), ((), ()))
WHOLE = pl.BlockSpec(memory_space=pltpu.VMEM)


def params(limit):
    return pltpu.CompilerParams(vmem_limit_bytes=limit * MIB)


def canonical(held, piece):
    if held is None:
        return piece
    chips, places = held
    me = lax.axis_index("control")
    shift, flip = places[piece]
    return (me // 2 + chips - shift) % chips * 2 + (me % 2 + flip) % 2


def log2_sum(parts):
    top = functools.reduce(jnp.maximum, parts)
    return top + jnp.log2(functools.reduce(jnp.add, [jnp.exp2(p - top) for p in parts]))


def turned(column):
    return jnp.transpose(jnp.broadcast_to(column, (128, 128)))[0:1, :]


def tree_sum(parts):
    while len(parts) > 1:
        parts = [functools.reduce(jnp.add, parts[i:i + 2]) for i in range(0, len(parts), 2)]
    return parts[0]


def folded(wide):
    return functools.reduce(jnp.add, [wide[:, j:j + 128] for j in range(0, wide.shape[1], 128)])


def scaled_product(x, y, scale):
    return lax.dot_general(x, y, NT_DIMS, preferred_element_type=jnp.float32) * scale


def chunk_kernel(scale, parts, earlier, held, *refs):
    x_refs, refs = refs[:parts], refs[parts:]
    y_ref, u_ref, refs = refs[0], refs[1], refs[2:]
    lse_refs, (e_ref, top_ref, lse_ref, wide_ref) = refs[:earlier], refs[earlier:]
    columns = y_ref.shape[0]
    x = jnp.concatenate([r[...] for r in x_refs], axis=0)
    rows = x.shape[0]
    tile = 256
    before = [r[h:h + 1, :] for r in lse_refs for h in range(r.shape[0])]

    def emit(top, total):
        own, sums = [], []
        for h in range(0, rows, 128):
            shift = turned(top[h:h + 128])
            row = jnp.sum(jnp.transpose(total[h:h + 128]), axis=0, keepdims=True)
            top_ref[h // 128:h // 128 + 1, :] = shift
            own.append(shift + jnp.log2(row))
            sums.append(row)
        for h, row in enumerate(before + own):
            if earlier:
                lse_ref[pl.ds(canonical(held, h), 1), :] = row
            else:
                lse_ref[h:h + 1, :] = row
        return functools.reduce(jnp.maximum, sums)

    top, total = None, None
    for j in range(0, columns, tile):
        t = scaled_product(x, y_ref[j:j + tile, :], scale) + u_ref[:, j:j + tile]
        if top is None:
            top = jnp.max(t, axis=1, keepdims=True)
        e = jnp.exp2(t - top)
        e_ref[:, j:j + tile] = e
        total = folded(e) if total is None else total + folded(e)
    largest = emit(top, total)

    @pl.when(jnp.logical_not(jnp.max(largest) < LARGE))
    def _():
        def scores(j):
            place = pl.ds(pl.multiple_of(j * tile, tile), tile)
            return place, scaled_product(x, y_ref[place, :], scale) + u_ref[:, place]

        wide_ref[...] = jnp.full_like(wide_ref, -jnp.inf)

        @pl.loop(0, columns // tile)
        def _(j):
            wide_ref[...] = jnp.maximum(wide_ref[...], jnp.max(scores(j)[1], axis=1, keepdims=True))

        top = wide_ref[:, 0:1]
        wide_ref[...] = jnp.zeros_like(wide_ref)

        @pl.loop(0, columns // tile)
        def _(j):
            place, t = scores(j)
            e = jnp.exp2(t - top)
            e_ref[:, place] = e
            wide_ref[...] += folded(e)

        emit(top, wide_ref[...])


def chunk_call(xs, y, u, held=None, lses=(), hidden=False):
    parts = len(xs)
    width = xs[0].shape[1]
    columns = y.shape[0]
    rows = sum(x.shape[0] for x in xs)
    scale = 2.0 * LOG2E / (width * smoothing)
    listed = rows // 128 + sum(a.shape[0] for a in lses)
    return pl.pallas_call(
        functools.partial(chunk_kernel, scale, parts, len(lses), held),
        in_specs=[WHOLE] * (parts + 2 + len(lses)),
        out_specs=[WHOLE, WHOLE, WHOLE],
        out_shape=[
            jax.ShapeDtypeStruct((rows, columns), jnp.float32),
            jax.ShapeDtypeStruct((rows // 128, 128), jnp.float32),
            jax.ShapeDtypeStruct((listed, 128), jnp.float32),
        ],
        scratch_shapes=[pltpu.VMEM((rows, 128), jnp.float32)],
        compiler_params=params(16),
        cost_estimate=pl.CostEstimate(
            flops=0 if hidden else 2 * rows * columns * width,
            bytes_accessed=0 if hidden else 2 * (rows + columns) * width + 4 * rows * columns,
            transcendentals=0 if hidden else rows * columns,
        ),
        name="chunk_scores",
    )(*xs, y, u, *lses)


def halves_kernel(count, *refs):
    for x_ref, first_ref, second_ref in zip(refs[:count], refs[count::2], refs[count + 1::2]):
        half = first_ref.shape[0]
        first_ref[...] = x_ref[:half, :]
        second_ref[...] = x_ref[half:, :]


def halves_call(xs):
    half = jax.ShapeDtypeStruct((xs[0].shape[0] // 2, xs[0].shape[1]), xs[0].dtype)
    return pl.pallas_call(
        functools.partial(halves_kernel, len(xs)),
        in_specs=[WHOLE] * len(xs),
        out_specs=[WHOLE] * (2 * len(xs)),
        out_shape=[half] * (2 * len(xs)),
        compiler_params=params(4),
        cost_estimate=pl.CostEstimate(flops=0, bytes_accessed=0, transcendentals=0),
        name="halves",
    )(*xs)


def merge_kernel(first_ref, second_ref, out_ref):
    out_ref[...] = log2_sum([first_ref[...], second_ref[...]])


def share_kernel(own_ref, near_ref, far_ref, out_ref):
    far = far_ref[...]
    out_ref[...] = jnp.where(lax.axis_index("control") % 2 == 0, log2_sum([own_ref[...], near_ref[...], far]), far)


def share_call(own, near, far):
    return pl.pallas_call(
        share_kernel,
        in_specs=[WHOLE] * 3,
        out_specs=WHOLE,
        out_shape=jax.ShapeDtypeStruct(own.shape, jnp.float32),
        compiler_params=params(1),
        cost_estimate=pl.CostEstimate(flops=8 * own.size, bytes_accessed=16 * own.size, transcendentals=0),
        name="share_rows",
    )(own, near, far)


def merge_call(first, second):
    return pl.pallas_call(
        merge_kernel,
        in_specs=[WHOLE, WHOLE],
        out_specs=WHOLE,
        out_shape=jax.ShapeDtypeStruct(first.shape, jnp.float32),
        compiler_params=params(1),
        cost_estimate=pl.CostEstimate(flops=8 * first.size, bytes_accessed=12 * first.size, transcendentals=0),
        name="merge_rows",
    )(first, second)


def weight_kernel(count, held, *refs):
    top_refs, (stat_ref, logw_ref, base_ref, most_ref) = refs[:count], refs[count:]
    at = 0
    for top_ref in top_refs:
        for r in range(top_ref.shape[0]):
            base_ref[pl.ds(canonical(held, at), 1), :] = top_ref[r:r + 1, :]
            at += 1
    base = base_ref[...] + logw_ref[...] * LOG2E
    bound = base - stat_ref[...]
    most = jnp.max(jnp.max(bound, axis=0, keepdims=True), axis=1, keepdims=True)
    base_ref[...] = base - most
    most_ref[...] = jnp.broadcast_to(most, most_ref.shape)


def weight_call(held, tops, stat, logw):
    shape = jax.ShapeDtypeStruct(stat.shape, jnp.float32)
    return pl.pallas_call(
        functools.partial(weight_kernel, len(tops), held),
        in_specs=[WHOLE] * (len(tops) + 2),
        out_specs=[WHOLE, WHOLE],
        out_shape=[shape, shape],
        compiler_params=params(1),
        cost_estimate=pl.CostEstimate(flops=8 * stat.size, bytes_accessed=16 * stat.size, transcendentals=0),
        name="row_weights",
    )(*tops, stat, logw)


def column_kernel(scale, counts, held, *refs):
    refs = list(refs)
    stat_refs, e_refs, x_refs = [[refs.pop(0) for _ in range(n)] for n in counts]
    base_ref, most_ref, logw_ref, u_ref, y_ref, out_ref, total_ref, v_ref, wide_ref, score_ref = refs
    columns = u_ref.shape[1]
    stats = [r[...] for r in stat_refs]
    top = functools.reduce(jnp.maximum, stats)
    share = functools.reduce(jnp.add, [jnp.exp2(p - top) for p in stats])
    most = most_ref[0:1, :]

    count = base_ref.shape[0]
    part_row = lax.broadcasted_iota(jnp.int32, (4 * count, 128 * count), 0)
    lane_row = lax.broadcasted_iota(jnp.int32, (4 * count, 128 * count), 1) // 128
    pattern = jnp.where(part_row % count == lane_row, 1.0, 0.0).astype(jnp.bfloat16)

    def spread(rows):
        parts = []
        for _ in range(3):
            parts.append(rows.astype(jnp.bfloat16).astype(jnp.float32))
            rows = rows - parts[-1]
        parts = jnp.concatenate(parts + [jnp.zeros_like(rows)], axis=0).astype(jnp.bfloat16)
        laid = lax.dot_general(parts, pattern, (((0,), (0,)), ((), ())), preferred_element_type=jnp.float32)
        for r in range(count):
            wide_ref[r * 128:(r + 1) * 128, :] = laid[:, r * 128:(r + 1) * 128]

    spread(jnp.exp2(base_ref[...] - top) / share)
    total_ref[...] = top + jnp.log2(share)
    starts = [sum(e.shape[0] for e in e_refs[:i]) // 128 for i in range(len(e_refs))]
    places = []
    for e_ref, start in zip(e_refs, starts):
        for r in range(0, e_ref.shape[0], 8):
            if r % 128 == 0:
                from_row = canonical(held, start + r // 128) * 128
            places.append((e_ref, r, pl.ds(pl.multiple_of(from_row + r % 128, 8), 8)))

    strips = columns // 128
    sums = [[] for _ in range(strips)]
    for first in range(0, len(places), 2):
        group = places[first:first + 2]
        weights = [wide_ref[at, :] for _, _, at in group]
        for s, part in enumerate(sums):
            terms = [e_ref[r:r + 8, s * 128:(s + 1) * 128] * a for (e_ref, r, _), a in zip(group, weights)]
            part[:] = [tree_sum(part + [tree_sum(terms)])]
    rows = jnp.concatenate([jnp.sum(part[0], axis=0, keepdims=True) for part in sums], axis=0)
    shifts = jnp.concatenate([u_ref[:, s * 128:(s + 1) * 128] for s in range(strips)], axis=0)
    out_ref[...] = jnp.log2(rows) + (most - shifts)
    least = jnp.min(rows, axis=0, keepdims=True)

    @pl.when(jnp.logical_not(jnp.min(least) > SMALL))
    def _():
        v_ref[...] = logw_ref[...] * LOG2E - total_ref[...]
        spread(v_ref[...])

        @pl.loop(0, columns // 128)
        def _(strip):
            y = y_ref[pl.ds(pl.multiple_of(strip * 128, 128), 128), :]
            at = 0
            for x_ref in x_refs:
                span = slice(at, at + x_ref.shape[0])
                from_row = canonical(held, at // 128) * 128 + at % 128
                v = wide_ref[pl.ds(pl.multiple_of(from_row, 8), x_ref.shape[0]), :]
                score_ref[span, :] = scaled_product(x_ref[...], y, scale) + v
                at += x_ref.shape[0]
            top = jnp.max(score_ref[...], axis=0, keepdims=True)
            row = jnp.sum(jnp.exp2(score_ref[...] - top), axis=0, keepdims=True)
            out_ref[pl.ds(strip, 1), :] = top + jnp.log2(row)


def column_call(held, stats, exps, pieces, base, most, logw, u, y):
    first = stats[0]
    columns, width = y.shape
    rows = 128 * first.shape[0]
    lists = [stats, exps, pieces]
    scale = 2.0 * LOG2E / (width * smoothing)
    return pl.pallas_call(
        functools.partial(column_kernel, scale, [len(part) for part in lists], held),
        in_specs=[WHOLE] * (sum(len(part) for part in lists) + 5),
        out_specs=[WHOLE, WHOLE],
        out_shape=[
            jax.ShapeDtypeStruct((columns // 128, 128), jnp.float32),
            jax.ShapeDtypeStruct(first.shape, jnp.float32),
        ],
        scratch_shapes=[
            pltpu.VMEM(first.shape, jnp.float32),
            pltpu.VMEM((rows, 128), jnp.float32),
            pltpu.VMEM((rows, 128), jnp.float32),
        ],
        compiler_params=params(20),
        cost_estimate=pl.CostEstimate(
            flops=2 * rows * columns,
            bytes_accessed=4 * rows * columns,
            transcendentals=0,
        ),
        name="column_lse",
    )(*stats, *exps, *pieces, base, most, logw, u, y)


def pot_kernel(inverse, held, parts, total_ref, *refs):
    x_refs, pot_ref = refs[:parts], refs[parts]
    squares = []
    for x_ref in x_refs:
        squares.append(folded(jnp.square(x_ref[...].astype(jnp.float32))))
    squares = jnp.concatenate(squares, axis=0)
    for h in range(squares.shape[0] // 128):
        norm = jnp.sum(jnp.transpose(squares[h * 128:(h + 1) * 128]), axis=0, keepdims=True)
        row = pl.ds(canonical(held, h), 1)
        pot_ref[row, :] = norm * inverse - total_ref[row, :] * LN2


def pot_call(held, total, pieces, inverse):
    return pl.pallas_call(
        functools.partial(pot_kernel, inverse, held, len(pieces)),
        in_specs=[WHOLE] * (1 + len(pieces)),
        out_specs=WHOLE,
        out_shape=jax.ShapeDtypeStruct(total.shape, jnp.float32),
        compiler_params=params(12),
        cost_estimate=pl.CostEstimate(
            flops=2 * sum(x.size for x in pieces),
            bytes_accessed=2 * sum(x.size for x in pieces),
            transcendentals=0,
        ),
        name="treated_pot",
    )(total, *pieces)


def body(chips, treated_emb, control_emb, control_pot, control_logw, treated_logw):
    width = control_emb.shape[1]
    inverse = 1.0 / (width * smoothing)
    control_sq = jnp.sum(jnp.square(control_emb.astype(jnp.float32)), axis=1) * inverse
    u = ((control_pot + control_logw - control_sq) * LOG2E)[None, :]
    logw = treated_logw.reshape(-1, 128)
    rows = treated_emb.shape[0]
    ring = chips == 4 and rows == 128

    def moved(value, target):
        perm = [(z * 2 + c, target(z, c)) for z in range(chips) for c in range(2)]
        return lax.ppermute(value, "control", perm)

    def swapped(value):
        return moved(value, lambda z, c: z * 2 + 1 - c)

    def shifted(value, shift):
        return moved(value, lambda z, c: (z + shift) % chips * 2 + c)

    if ring:
        held = (chips, ((0, 0), (0, 1), (1, 0), (1, 1), (3, 0), (3, 1), (2, 0), (2, 1)))
        x0 = treated_emb
        x1 = shifted(x0, 1)
        p0 = swapped(x0)
        behind, u = lax.optimization_barrier((x0, u))
        x3 = shifted(behind, 3)
        e0, top0, lse0 = chunk_call([x0, p0], control_emb, u)
        x1, lse0 = lax.optimization_barrier((x1, lse0))
        x2 = shifted(x1, 1)
        p1 = [swapped(part) for part in halves_call([x1])]
        e1, top1, lse1 = chunk_call([x1, *p1], control_emb, u, hidden=True)
        x3, lse1 = lax.optimization_barrier((x3, lse1))
        p3 = [swapped(part) for part in halves_call([x3])]
        e2, top2, lse2 = chunk_call([x3, *p3], control_emb, u, hidden=True)
        x2, lse2 = lax.optimization_barrier((x2, lse2))
        p2 = swapped(x2)
        e3, top3, stats = chunk_call([x2, p2], control_emb, u, held, [lse0, lse1, lse2])
        exps, tops = [e0, e1, e2, e3], [top0, top1, top2, top3]
        pieces = [x0, p0, x1, *p1, x3, *p3, x2, p2]
        chip_stats = merge_call(stats, swapped(stats))
        near = moved(chip_stats, lambda z, c: (z ^ 1) * 2 + c)
        far = moved(chip_stats, lambda z, c: (z ^ (2 + c)) * 2 + c)
        share = share_call(chip_stats, near, far)
        stats, bound = [share, swapped(share)], chip_stats
    else:
        held = None
        block = lax.all_gather(treated_emb, "control", axis=0, tiled=True)
        pieces = [block[i:i + 128] for i in range(0, block.shape[0], 128)]
        exps, tops, lses = [], [], []
        for k in range(0, len(pieces), 2):
            e, top, lse = chunk_call(pieces[k:k + 2], control_emb, u)
            exps.append(e)
            tops.append(top)
            lses.append(lse)
        gathered = lax.all_gather(jnp.concatenate(lses, axis=0), "control")
        top = jnp.max(gathered, axis=0)
        stats = [top + jnp.log2(jnp.sum(jnp.exp2(gathered - top[None]), axis=0))]
        bound = stats[0]

    if ring:
        pieces = list(lax.optimization_barrier((tuple(pieces), stats[-1]))[0])
    base, most = weight_call(held, tops, bound, logw)
    column, total = column_call(held, stats, exps, pieces, base, most, logw, u, control_emb)
    treated_pot = pot_call(held, total, pieces, inverse).reshape(-1)

    size = lax.axis_size("treated")
    if size == 4:
        parts = [column]
        for flip in (1, 2, 3):
            parts.append(lax.ppermute(column, "treated", [(s, s ^ flip) for s in range(size)]))
    else:
        gathered = lax.all_gather(column, "treated")
        parts = [gathered[s] for s in range(size)]
    column_lse = log2_sum(parts).reshape(-1) * LN2 - control_sq
    return (treated_pot, column_lse)


def solution(mesh):
    placed = (
        P(("treated", "control"), None),
        P("control", None),
        P("control"),
        P("control"),
        P("treated"),
    )
    return jax.shard_map(
        functools.partial(body, mesh.shape["control"] // 2),
        mesh=mesh,
        in_specs=placed,
        out_specs=(P("treated"), P("control")),
        check_vma=False,
    )
```

```python
import functools

import jax
import jax.numpy as jnp
from jax import lax
from jax.experimental import pallas as pl
from jax.experimental.pallas import tpu as pltpu
from jax.sharding import PartitionSpec as P

smoothing = 0.1
LOG2E = 1.4426950408889634
LN2 = 0.6931471805599453
LARGE = 2.0**30
SMALL = 2.0**-50
MIB = 1024 * 1024
NT_DIMS = (((1,), (1,)), ((), ()))
WHOLE = pl.BlockSpec(memory_space=pltpu.VMEM)


def params(limit):
    return pltpu.CompilerParams(vmem_limit_bytes=limit * MIB)


def canonical(held, piece):
    if held is None:
        return piece
    chips, places = held
    me = lax.axis_index("control")
    shift, flip = places[piece]
    return (me // 2 + chips - shift) % chips * 2 + (me % 2 + flip) % 2


def log2_sum(parts):
    top = functools.reduce(jnp.maximum, parts)
    return top + jnp.log2(functools.reduce(jnp.add, [jnp.exp2(p - top) for p in parts]))


def turned(column):
    return jnp.transpose(jnp.broadcast_to(column, (128, 128)))[0:1, :]


def tree_sum(parts):
    while len(parts) > 1:
        parts = [functools.reduce(jnp.add, parts[i:i + 2]) for i in range(0, len(parts), 2)]
    return parts[0]


def folded(wide):
    return functools.reduce(jnp.add, [wide[:, j:j + 128] for j in range(0, wide.shape[1], 128)])


def scaled_product(x, y, scale):
    return lax.dot_general(x, y, NT_DIMS, preferred_element_type=jnp.float32) * scale


def chunk_kernel(scale, parts, earlier, held, *refs):
    x_refs, refs = refs[:parts], refs[parts:]
    y_ref, u_ref, refs = refs[0], refs[1], refs[2:]
    lse_refs, (e_ref, top_ref, lse_ref, wide_ref) = refs[:earlier], refs[earlier:]
    columns = y_ref.shape[0]
    x = jnp.concatenate([r[...] for r in x_refs], axis=0)
    rows = x.shape[0]
    tile = 256
    before = [r[h:h + 1, :] for r in lse_refs for h in range(r.shape[0])]

    def emit(top, total):
        own, sums = [], []
        for h in range(0, rows, 128):
            shift = turned(top[h:h + 128])
            row = jnp.sum(jnp.transpose(total[h:h + 128]), axis=0, keepdims=True)
            top_ref[h // 128:h // 128 + 1, :] = shift
            own.append(shift + jnp.log2(row))
            sums.append(row)
        for h, row in enumerate(before + own):
            if earlier:
                lse_ref[pl.ds(canonical(held, h), 1), :] = row
            else:
                lse_ref[h:h + 1, :] = row
        return functools.reduce(jnp.maximum, sums)

    top, total = None, None
    for j in range(0, columns, tile):
        t = scaled_product(x, y_ref[j:j + tile, :], scale) + u_ref[:, j:j + tile]
        if top is None:
            top = jnp.max(t, axis=1, keepdims=True)
        e = jnp.exp2(t - top)
        e_ref[:, j:j + tile] = e
        total = folded(e) if total is None else total + folded(e)
    largest = emit(top, total)

    @pl.when(jnp.logical_not(jnp.max(largest) < LARGE))
    def _():
        def scores(j):
            place = pl.ds(pl.multiple_of(j * tile, tile), tile)
            return place, scaled_product(x, y_ref[place, :], scale) + u_ref[:, place]

        wide_ref[...] = jnp.full_like(wide_ref, -jnp.inf)

        @pl.loop(0, columns // tile)
        def _(j):
            wide_ref[...] = jnp.maximum(wide_ref[...], jnp.max(scores(j)[1], axis=1, keepdims=True))

        top = wide_ref[:, 0:1]
        wide_ref[...] = jnp.zeros_like(wide_ref)

        @pl.loop(0, columns // tile)
        def _(j):
            place, t = scores(j)
            e = jnp.exp2(t - top)
            e_ref[:, place] = e
            wide_ref[...] += folded(e)

        emit(top, wide_ref[...])


def chunk_call(xs, y, u, held=None, lses=(), hidden=False):
    parts = len(xs)
    width = xs[0].shape[1]
    columns = y.shape[0]
    rows = sum(x.shape[0] for x in xs)
    scale = 2.0 * LOG2E / (width * smoothing)
    listed = rows // 128 + sum(a.shape[0] for a in lses)
    return pl.pallas_call(
        functools.partial(chunk_kernel, scale, parts, len(lses), held),
        in_specs=[WHOLE] * (parts + 2 + len(lses)),
        out_specs=[WHOLE, WHOLE, WHOLE],
        out_shape=[
            jax.ShapeDtypeStruct((rows, columns), jnp.float32),
            jax.ShapeDtypeStruct((rows // 128, 128), jnp.float32),
            jax.ShapeDtypeStruct((listed, 128), jnp.float32),
        ],
        scratch_shapes=[pltpu.VMEM((rows, 128), jnp.float32)],
        compiler_params=params(16),
        cost_estimate=pl.CostEstimate(
            flops=0 if hidden else 2 * rows * columns * width,
            bytes_accessed=0 if hidden else 2 * (rows + columns) * width + 4 * rows * columns,
            transcendentals=0 if hidden else rows * columns,
        ),
        name="chunk_scores",
    )(*xs, y, u, *lses)


def halves_kernel(count, *refs):
    for x_ref, first_ref, second_ref in zip(refs[:count], refs[count::2], refs[count + 1::2]):
        half = first_ref.shape[0]
        first_ref[...] = x_ref[:half, :]
        second_ref[...] = x_ref[half:, :]


def halves_call(xs):
    half = jax.ShapeDtypeStruct((xs[0].shape[0] // 2, xs[0].shape[1]), xs[0].dtype)
    return pl.pallas_call(
        functools.partial(halves_kernel, len(xs)),
        in_specs=[WHOLE] * len(xs),
        out_specs=[WHOLE] * (2 * len(xs)),
        out_shape=[half] * (2 * len(xs)),
        compiler_params=params(4),
        cost_estimate=pl.CostEstimate(flops=0, bytes_accessed=0, transcendentals=0),
        name="halves",
    )(*xs)


def merge_kernel(first_ref, second_ref, out_ref):
    out_ref[...] = log2_sum([first_ref[...], second_ref[...]])


def share_kernel(own_ref, first_ref, second_ref, out_ref):
    other = jnp.where(lax.axis_index("control") % 2 == 0, own_ref[...], second_ref[...])
    out_ref[...] = log2_sum([first_ref[...], other])


def share_call(own, first, second):
    return pl.pallas_call(
        share_kernel,
        in_specs=[WHOLE] * 3,
        out_specs=WHOLE,
        out_shape=jax.ShapeDtypeStruct(own.shape, jnp.float32),
        compiler_params=params(1),
        cost_estimate=pl.CostEstimate(flops=8 * own.size, bytes_accessed=16 * own.size, transcendentals=0),
        name="share_rows",
    )(own, first, second)


def merge_call(first, second):
    return pl.pallas_call(
        merge_kernel,
        in_specs=[WHOLE, WHOLE],
        out_specs=WHOLE,
        out_shape=jax.ShapeDtypeStruct(first.shape, jnp.float32),
        compiler_params=params(1),
        cost_estimate=pl.CostEstimate(flops=8 * first.size, bytes_accessed=12 * first.size, transcendentals=0),
        name="merge_rows",
    )(first, second)


def weight_kernel(count, held, *refs):
    top_refs, (stat_ref, logw_ref, base_ref, most_ref) = refs[:count], refs[count:]
    at = 0
    for top_ref in top_refs:
        for r in range(top_ref.shape[0]):
            base_ref[pl.ds(canonical(held, at), 1), :] = top_ref[r:r + 1, :]
            at += 1
    base = base_ref[...] + logw_ref[...] * LOG2E
    bound = base - stat_ref[...]
    most = jnp.max(jnp.max(bound, axis=0, keepdims=True), axis=1, keepdims=True)
    base_ref[...] = base - most
    most_ref[...] = jnp.broadcast_to(most, most_ref.shape)


def weight_call(held, tops, stat, logw):
    shape = jax.ShapeDtypeStruct(stat.shape, jnp.float32)
    return pl.pallas_call(
        functools.partial(weight_kernel, len(tops), held),
        in_specs=[WHOLE] * (len(tops) + 2),
        out_specs=[WHOLE, WHOLE],
        out_shape=[shape, shape],
        compiler_params=params(1),
        cost_estimate=pl.CostEstimate(flops=8 * stat.size, bytes_accessed=16 * stat.size, transcendentals=0),
        name="row_weights",
    )(*tops, stat, logw)


def column_kernel(scale, counts, held, *refs):
    refs = list(refs)
    stat_refs, e_refs, x_refs = [[refs.pop(0) for _ in range(n)] for n in counts]
    base_ref, most_ref, logw_ref, u_ref, y_ref, out_ref, total_ref, v_ref, wide_ref, score_ref = refs
    columns = u_ref.shape[1]
    stats = [r[...] for r in stat_refs]
    top = functools.reduce(jnp.maximum, stats)
    share = functools.reduce(jnp.add, [jnp.exp2(p - top) for p in stats])
    most = most_ref[0:1, :]

    count = base_ref.shape[0]
    part_row = lax.broadcasted_iota(jnp.int32, (4 * count, 128 * count), 0)
    lane_row = lax.broadcasted_iota(jnp.int32, (4 * count, 128 * count), 1) // 128
    pattern = jnp.where(part_row % count == lane_row, 1.0, 0.0).astype(jnp.bfloat16)

    def spread(rows):
        parts = []
        for _ in range(3):
            parts.append(rows.astype(jnp.bfloat16).astype(jnp.float32))
            rows = rows - parts[-1]
        parts = jnp.concatenate(parts + [jnp.zeros_like(rows)], axis=0).astype(jnp.bfloat16)
        laid = lax.dot_general(parts, pattern, (((0,), (0,)), ((), ())), preferred_element_type=jnp.float32)
        for r in range(count):
            wide_ref[r * 128:(r + 1) * 128, :] = laid[:, r * 128:(r + 1) * 128]

    spread(jnp.exp2(base_ref[...] - top) / share)
    total_ref[...] = top + jnp.log2(share)
    starts = [sum(e.shape[0] for e in e_refs[:i]) // 128 for i in range(len(e_refs))]
    places = []
    for e_ref, start in zip(e_refs, starts):
        for r in range(0, e_ref.shape[0], 8):
            if r % 128 == 0:
                from_row = canonical(held, start + r // 128) * 128
            places.append((e_ref, r, pl.ds(pl.multiple_of(from_row + r % 128, 8), 8)))

    strips = columns // 128
    sums = [[] for _ in range(strips)]
    for first in range(0, len(places), 2):
        group = places[first:first + 2]
        weights = [wide_ref[at, :] for _, _, at in group]
        for s, part in enumerate(sums):
            terms = [e_ref[r:r + 8, s * 128:(s + 1) * 128] * a for (e_ref, r, _), a in zip(group, weights)]
            part[:] = [tree_sum(part + [tree_sum(terms)])]
    rows = jnp.concatenate([jnp.sum(part[0], axis=0, keepdims=True) for part in sums], axis=0)
    shifts = jnp.concatenate([u_ref[:, s * 128:(s + 1) * 128] for s in range(strips)], axis=0)
    out_ref[...] = jnp.log2(rows) + (most - shifts)
    least = jnp.min(rows, axis=0, keepdims=True)

    @pl.when(jnp.logical_not(jnp.min(least) > SMALL))
    def _():
        v_ref[...] = logw_ref[...] * LOG2E - total_ref[...]
        spread(v_ref[...])

        @pl.loop(0, columns // 128)
        def _(strip):
            y = y_ref[pl.ds(pl.multiple_of(strip * 128, 128), 128), :]
            at = 0
            for x_ref in x_refs:
                span = slice(at, at + x_ref.shape[0])
                from_row = canonical(held, at // 128) * 128 + at % 128
                v = wide_ref[pl.ds(pl.multiple_of(from_row, 8), x_ref.shape[0]), :]
                score_ref[span, :] = scaled_product(x_ref[...], y, scale) + v
                at += x_ref.shape[0]
            top = jnp.max(score_ref[...], axis=0, keepdims=True)
            row = jnp.sum(jnp.exp2(score_ref[...] - top), axis=0, keepdims=True)
            out_ref[pl.ds(strip, 1), :] = top + jnp.log2(row)


def column_call(held, stats, exps, pieces, base, most, logw, u, y):
    first = stats[0]
    columns, width = y.shape
    rows = 128 * first.shape[0]
    lists = [stats, exps, pieces]
    scale = 2.0 * LOG2E / (width * smoothing)
    return pl.pallas_call(
        functools.partial(column_kernel, scale, [len(part) for part in lists], held),
        in_specs=[WHOLE] * (sum(len(part) for part in lists) + 5),
        out_specs=[WHOLE, WHOLE],
        out_shape=[
            jax.ShapeDtypeStruct((columns // 128, 128), jnp.float32),
            jax.ShapeDtypeStruct(first.shape, jnp.float32),
        ],
        scratch_shapes=[
            pltpu.VMEM(first.shape, jnp.float32),
            pltpu.VMEM((rows, 128), jnp.float32),
            pltpu.VMEM((rows, 128), jnp.float32),
        ],
        compiler_params=params(20),
        cost_estimate=pl.CostEstimate(
            flops=2 * rows * columns,
            bytes_accessed=4 * rows * columns,
            transcendentals=0,
        ),
        name="column_lse",
    )(*stats, *exps, *pieces, base, most, logw, u, y)


def pot_kernel(inverse, held, parts, total_ref, *refs):
    x_refs, pot_ref = refs[:parts], refs[parts]
    squares = []
    for x_ref in x_refs:
        squares.append(folded(jnp.square(x_ref[...].astype(jnp.float32))))
    squares = jnp.concatenate(squares, axis=0)
    for h in range(squares.shape[0] // 128):
        norm = jnp.sum(jnp.transpose(squares[h * 128:(h + 1) * 128]), axis=0, keepdims=True)
        row = pl.ds(canonical(held, h), 1)
        pot_ref[row, :] = norm * inverse - total_ref[row, :] * LN2


def pot_call(held, total, pieces, inverse):
    return pl.pallas_call(
        functools.partial(pot_kernel, inverse, held, len(pieces)),
        in_specs=[WHOLE] * (1 + len(pieces)),
        out_specs=WHOLE,
        out_shape=jax.ShapeDtypeStruct(total.shape, jnp.float32),
        compiler_params=params(12),
        cost_estimate=pl.CostEstimate(
            flops=2 * sum(x.size for x in pieces),
            bytes_accessed=2 * sum(x.size for x in pieces),
            transcendentals=0,
        ),
        name="treated_pot",
    )(total, *pieces)


def body(chips, treated_emb, control_emb, control_pot, control_logw, treated_logw):
    width = control_emb.shape[1]
    inverse = 1.0 / (width * smoothing)
    control_sq = jnp.sum(jnp.square(control_emb.astype(jnp.float32)), axis=1) * inverse
    u = ((control_pot + control_logw - control_sq) * LOG2E)[None, :]
    logw = treated_logw.reshape(-1, 128)
    rows = treated_emb.shape[0]
    ring = chips == 4 and rows == 128

    def moved(value, target):
        perm = [(z * 2 + c, target(z, c)) for z in range(chips) for c in range(2)]
        return lax.ppermute(value, "control", perm)

    def swapped(value):
        return moved(value, lambda z, c: z * 2 + 1 - c)

    def shifted(value, shift):
        return moved(value, lambda z, c: (z + shift) % chips * 2 + c)

    if ring:
        held = (chips, ((0, 0), (0, 1), (1, 0), (1, 1), (3, 0), (3, 1), (2, 0), (2, 1)))
        x0 = treated_emb
        x1 = shifted(x0, 1)
        p0 = swapped(x0)
        behind, u = lax.optimization_barrier((x0, u))
        x3 = shifted(behind, 3)
        e0, top0, lse0 = chunk_call([x0, p0], control_emb, u)
        x1, lse0 = lax.optimization_barrier((x1, lse0))
        x2 = shifted(x1, 1)
        p1 = [swapped(part) for part in halves_call([x1])]
        e1, top1, lse1 = chunk_call([x1, *p1], control_emb, u, hidden=True)
        x3, lse1 = lax.optimization_barrier((x3, lse1))
        p3 = [swapped(part) for part in halves_call([x3])]
        e2, top2, lse2 = chunk_call([x3, *p3], control_emb, u, hidden=True)
        x2, lse2 = lax.optimization_barrier((x2, lse2))
        p2 = swapped(x2)
        e3, top3, stats = chunk_call([x2, p2], control_emb, u, held, [lse0, lse1, lse2])
        exps, tops = [e0, e1, e2, e3], [top0, top1, top2, top3]
        pieces = [x0, p0, x1, *p1, x3, *p3, x2, p2]
        chip_stats = merge_call(stats, swapped(stats))
        second = moved(chip_stats, lambda z, c: (z ^ (1 + c)) * 2 + c)
        first = moved(chip_stats, lambda z, c: (z ^ (1 + 2 * c)) * 2 + c)
        share = share_call(chip_stats, first, second)
        stats, bound = [share, swapped(share)], chip_stats
    else:
        held = None
        block = lax.all_gather(treated_emb, "control", axis=0, tiled=True)
        pieces = [block[i:i + 128] for i in range(0, block.shape[0], 128)]
        exps, tops, lses = [], [], []
        for k in range(0, len(pieces), 2):
            e, top, lse = chunk_call(pieces[k:k + 2], control_emb, u)
            exps.append(e)
            tops.append(top)
            lses.append(lse)
        gathered = lax.all_gather(jnp.concatenate(lses, axis=0), "control")
        top = jnp.max(gathered, axis=0)
        stats = [top + jnp.log2(jnp.sum(jnp.exp2(gathered - top[None]), axis=0))]
        bound = stats[0]

    if ring:
        pieces = list(lax.optimization_barrier((tuple(pieces), stats[-1]))[0])
    base, most = weight_call(held, tops, bound, logw)
    column, total = column_call(held, stats, exps, pieces, base, most, logw, u, control_emb)
    treated_pot = pot_call(held, total, pieces, inverse).reshape(-1)

    size = lax.axis_size("treated")
    if size == 4:
        parts = [column]
        for flip in (1, 2, 3):
            parts.append(lax.ppermute(column, "treated", [(s, s ^ flip) for s in range(size)]))
    else:
        gathered = lax.all_gather(column, "treated")
        parts = [gathered[s] for s in range(size)]
    column_lse = log2_sum(parts).reshape(-1) * LN2 - control_sq
    return (treated_pot, column_lse)


def solution(mesh):
    placed = (
        P(("treated", "control"), None),
        P("control", None),
        P("control"),
        P("control"),
        P("treated"),
    )
    return jax.shard_map(
        functools.partial(body, mesh.shape["control"] // 2),
        mesh=mesh,
        in_specs=placed,
        out_specs=(P("treated"), P("control")),
        check_vma=False,
    )
```
